256 devices in a mesh: group: 4 (over y), shard: 64 (over z, x, core).
Axes of the slice: x: 4, y: 4, z: 8, core: 2. Of those that a mesh axis runs over, the one named last changes fastest.
Arguments:
- queries: bfloat16 [2048, 32, 128], P('shard', 'group'), may hold values from -1.75 to 1.75
- passages: bfloat16 [16384, 64, 128], P(('group', 'shard')), may hold values from -1.75 to 1.75
- lengths: int32 [16384], P(('group', 'shard')), may hold values from 8 to 64
- target_shard: int32 [4, 2048, 8], P('group', 'shard'), may hold values from 0 to 63, all different within a row; in each aligned block of 32 rows (0 to 31, 32 to 63, ..., all dimensions but the last counted through in order) at most 6 rows name the same one
- passage_slot: int32 [4, 2048, 8, 16], P('group', 'shard'), may hold values from 0 to 63
Outputs:
- scores: float32 [4, 2048, 8, 16], P('group', 'shard')
The draws below stay inside these ranges and needn't reach their ends.
Inputs may be any that keep to these rules, and one draw needn't show every extreme that they name: `target_shard`: each row names 8 different shards; within the rows of one device no shard is named more than 6 times, a bound that some block reaches.
All inputs are finite; a program needn't handle non-finite values.
Results may differ from the reference program's by a relative error of at most 0.0003.
Values may be sent and summed in bfloat16 or wider, within the bound.
No kernel may reach another device: no remote copies, remote signals or barrier semaphores. Data moves between devices by JAX's collectives and lax.ppermute only.
A program may use at most 64 MiB of HBM per device.

```python
import math
import jax
import jax.numpy as jnp
import numpy as np
from jax import lax

DIM = 128
LQ = 32
LP = 64
B = 8
K = 16
QDEV = 32
P_DEV = 64
GROUPS = 4
Q = 2048
CAP = 6
PASSAGES = 16384
N_SHARD = 64


def place_ends(entries, stream_key, low, top_value):
    extent = entries.shape
    place = [jax.random.randint(jax.random.fold_in(stream_key, axis), (), 0, extent[axis]) for axis in range(len(extent))]
    entries = entries.at[tuple(place)].set(low)
    longest = extent.index(max(extent))
    place[longest] = (place[longest] + 1) % extent[longest]
    return entries.at[tuple(place)].set(top_value)


def levels(key, dims, shards, low, top_value):
    factor_of = 1.0
    for position, parts in shards:
        draws = jax.random.uniform(jax.random.fold_in(jax.random.fold_in(key, 6), position), (parts,), jnp.float32, low / len(shards), top_value / len(shards))
        factor_of = factor_of * jnp.repeat(jnp.exp(draws), dims[position] // parts).reshape((-1,) + (1,) * (len(dims) - 1 - position))
    return factor_of


def shared_out(key, own, number, rows, count, top, reach, skew):
    sequence = jax.random.permutation(key, count)
    packed, ordinary = load_shares(count, rows * top, reach, skew, True), load_shares(count, rows * top, reach, skew, False)
    places = jnp.arange(count)

    def named(sizes, turn):
        used = int((sizes > 0).sum())
        fixed = max(1, used // 4)
        passed = fixed + (places - fixed + turn * (used - fixed)) % max(1, count - fixed)
        return jnp.zeros((count,), jnp.int32).at[sequence[jnp.where(places < fixed, places, passed)]].set(jnp.asarray(sizes, jnp.int32))

    sizes = jnp.where(number % 4 == 0, named(packed, number // 4), named(ordinary, number - number // 4 - 1))
    mixed = jax.random.permutation(jax.random.fold_in(own, 3), count)
    donor, taker = mixed[0:count // 2 * 2:2], mixed[1:count // 2 * 2:2]
    room = jnp.minimum(sizes[donor] - 1, reach - sizes[taker]) // 2
    room = jnp.where((donor == sequence[0]) | (taker == sequence[0]) | (sizes[taker] == 0), 0, jnp.maximum(room, 0))
    passed = jax.random.randint(jax.random.fold_in(own, 4), (count // 2,), 0, 1 << 20) % (room + 1)
    sizes = sizes.at[donor].add(-passed).at[taker].add(passed)
    members = jnp.searchsorted(jnp.cumsum(sizes), jnp.arange(rows * top), side="right").astype(jnp.int32)
    listing = members.reshape(top, rows).T
    listing = listing[jax.random.permutation(jax.random.fold_in(own, 1), rows)]
    turn = jax.random.randint(jax.random.fold_in(own, 2), (rows, 1), 0, top)
    return jnp.take_along_axis(listing, (jnp.arange(top)[None, :] + turn) % top, axis=1)


def load_shares(number_of, total, most, lean, full):
    portions = [(1 << 20) // math.isqrt(grade ** lean) + 1 for grade in range(1, number_of + 1)]
    largest = most if full else min(most, max(-(-total // number_of), total * portions[0] // sum(portions)))
    least = 1 if total - largest >= number_of - 1 else 0
    counts, rest = [largest] + [least] * (number_of - 1), total - largest - least * (number_of - 1)
    while rest > 0:
        free = [i for i in range(1, number_of) if counts[i] < largest] or [i for i in range(1, number_of) if counts[i] < most]
        whole, remaining = sum([portions[i] for i in free]), rest
        for i in free:
            addition = min(most - counts[i], max(1, remaining * portions[i] // whole), rest)
            counts[i] = counts[i] + addition
            rest = rest - addition
    return np.array(counts)


def scatter_about(key, extent, spread, bound, split=(), kind=jnp.bfloat16):
    entries = spread * jax.random.normal(key, extent, jnp.float32)
    if split:
        entries = entries * levels(key, extent, split, -0.22, 0.18)
    return jnp.clip(entries, -bound, bound).astype(kind)


def setup_inputs(seed: int = 0) -> dict:
    keys = jax.random.split(jax.random.key(seed), 6)
    queries = scatter_about(keys[0], (Q, LQ, DIM), 0.3, 1.75, ((0, 64), (1, 4)))
    passages = scatter_about(keys[1], (PASSAGES, LP, DIM), 0.3, 1.75, ((0, 256),))
    lengths = place_ends(jax.random.randint(keys[2], (PASSAGES,), LP // 8, LP + 1), jax.random.fold_in(keys[2], 1), LP // 8, LP).astype(jnp.int32)
    target_shard_keys = jax.random.split(jax.random.fold_in(keys[3], 1), GROUPS * Q // QDEV)
    target_shard_turns = jax.random.permutation(jax.random.fold_in(keys[3], 3), GROUPS * Q // QDEV)
    target_shard = jax.vmap(lambda own, number: shared_out(jax.random.fold_in(keys[3], 2), own, number, QDEV, N_SHARD, B, CAP, 2))(target_shard_keys, target_shard_turns).reshape((GROUPS, Q, B))
    passage_slot = place_ends(jax.random.randint(keys[4], (GROUPS, Q, B, K), 0, P_DEV), jax.random.fold_in(keys[4], 1), 0, P_DEV - 1).astype(jnp.int32)
    return {"queries": queries, "passages": passages, "lengths": lengths, "target_shard": target_shard, "passage_slot": passage_slot}


def reference(queries, passages, lengths, target_shard, passage_slot):
    group_ids = lax.broadcasted_iota(jnp.int32, (GROUPS, 1), 0)

    def one_query(member):
        tokens, target_row, slot_row = member
        ids = ((group_ids * N_SHARD + target_row)[..., None] * P_DEV + slot_row).astype(jnp.int32)
        flat_ids = ids.reshape(-1)
        chosen = passages[flat_ids].astype(jnp.float32)
        similar = jnp.einsum("td,cpd->tcp", tokens.astype(jnp.float32), chosen)
        positions = lax.broadcasted_iota(jnp.int32, (1, 1, LP), 2)
        limits = lengths[flat_ids]
        masked = jnp.where(positions < limits[None, :, None], similar, jnp.float32(-1e30))
        best = jnp.max(masked, axis=2)
        total = jnp.sum(best, axis=0) * jnp.float32(1.0 / LQ)
        return total.reshape(GROUPS, B, K)

    per_query = lax.map(one_query, (queries, jnp.transpose(target_shard, (1, 0, 2)), jnp.transpose(passage_slot, (1, 0, 2, 3))))
    return jnp.transpose(per_query, (1, 0, 2, 3))
```

```python
import functools
import jax
import jax.numpy as jnp
from jax import lax
from jax.experimental import pallas as pl
from jax.experimental.pallas import tpu as pltpu
from jax.sharding import Mesh, PartitionSpec as P

NZ, NX, NC = 8, 4, 2
RANKS = 6
NT = (((1,), (1,)), ((), ()))
ROW_LANE = 96
GROUP = 2
CHUNK = 512


def score_kernel(layout, sources, *refs):
    count = 1 + max(i for _, parts in layout for i in parts)
    table_s, ids, table_v = refs[:3]
    passages = refs[3:3 + count]
    near = refs[3 + count:3 + count + sources]
    far = refs[3 + count + sources:3 + count + 2 * sources]
    out, weights, best = refs[-3:]
    width = 32 * sources
    lane = lax.broadcasted_iota(jnp.int32, (sources, 128), 1)
    picks = (RANKS * sources, RANKS * width)
    ones = (lax.broadcasted_iota(jnp.int32, picks, 1) // 32
            == lax.broadcasted_iota(jnp.int32, picks, 0)).astype(jnp.bfloat16)
    best[...] = jnp.zeros_like(best)
    for place, parts in layout:
        block = ids[sources + place]
        origin = [ids[s] for s in range(sources)]
        rows = [[table_s[origin[s] * 8 + block, ROW_LANE + i] for s in range(sources)]
                for i in range(RANKS)]
        for i in range(RANKS):
            for s in range(sources):
                row = jnp.maximum(rows[i][s] - 1, 0)
                start = i * width + s * 32
                weights[start:start + 16, :] = near[s][row]
                weights[start + 16:start + 32, :] = far[s][row]
        for first in range(0, RANKS, GROUP):
            named = functools.reduce(lambda a, b: a + b, sum(rows[first:first + GROUP], []))
            low, high = first * width, (first + GROUP) * width

            @pl.when(named > 0)
            def _():
                tokens = weights[low:high, :]
                done = 0
                for part in parts:
                    for c in range(0, passages[part].shape[0], CHUNK):
                        similar = lax.dot_general(passages[part][c:c + CHUNK, :], tokens, NT,
                                                  preferred_element_type=jnp.float32)
                        top = jnp.max(similar.reshape(CHUNK // 64, 64, high - low), axis=1)
                        best[done:done + CHUNK // 64, low:high] = top
                        done += CHUNK // 64

        value = best[...]
        total = jnp.zeros((RANKS * sources, 64), jnp.float32)
        for _ in range(3):
            piece = value.astype(jnp.bfloat16)
            total += lax.dot_general(ones, piece, NT, preferred_element_type=jnp.float32)
            value = value - piece.astype(jnp.float32)
        total = total * jnp.float32(1.0 / 32)
        total = jnp.concatenate([total, total], axis=1)
        index = jnp.concatenate([table_v[origin[s], pl.ds(block, 1), :] for s in range(sources)], axis=0)
        index = jnp.bitwise_and(index, 63)
        result = jnp.zeros((sources, 128), jnp.float32)
        for i in range(RANKS):
            found = jnp.take_along_axis(total[i * sources:(i + 1) * sources], index, axis=1)
            result = jnp.where(lane // 16 == i, found, result)
        for s in range(sources):
            out[origin[s], pl.ds(block, 1), :] = result[s:s + 1]


def add_kernel(layout, sources, *refs):
    refs[-3][...] = refs[-4][...]
    score_kernel(layout, sources, *refs[:-4], *refs[-3:])


def score(layout, table, ids, passages, near, far, previous=None):
    sources = len(near)
    smem = pl.BlockSpec(memory_space=pltpu.SMEM)
    vmem = pl.BlockSpec(memory_space=pltpu.VMEM)
    operands = [table.reshape(64, 128), ids, table, *passages, *near, *far]
    specs = [smem, smem] + [vmem] * (len(operands) - 2)
    body = score_kernel
    aliases = {}
    if previous is not None:
        aliases = {len(operands): 0}
        operands.append(previous)
        specs.append(vmem)
        body = add_kernel
    live = len(layout) * 4096 * 32 * sources * RANKS
    return pl.pallas_call(
        functools.partial(body, layout, sources),
        in_specs=specs,
        out_specs=vmem,
        out_shape=jax.ShapeDtypeStruct((8, 8, 128), jnp.float32),
        scratch_shapes=[
            pltpu.VMEM((RANKS * 32 * sources, 128), jnp.bfloat16),
            pltpu.VMEM((64, RANKS * 32 * sources), jnp.float32),
        ],
        input_output_aliases=aliases,
        compiler_params=pltpu.CompilerParams(vmem_limit_bytes=40 * 2**20),
        cost_estimate=pl.CostEstimate(flops=2 * 128 * live, bytes_accessed=2**20, transcendentals=0),
    )(*operands)


def shift(value, axis, size, by):
    return lax.ppermute(value, axis, [(i, (i + by) % size) for i in range(size)])


def ring(near, far):
    up = [[near], [far]]
    down = [[near], [far]]
    for step in range(1, 5):
        for chunk in range(2):
            if step < 4 or chunk == 0:
                up[chunk].append(shift(up[chunk][-1], "z", NZ, 1))
            if step < 4 or chunk == 1:
                down[chunk].append(shift(down[chunk][-1], "z", NZ, -1))
    chunks = []
    for chunk in range(2):
        one = [up[chunk][0]]
        for step in range(1, 4):
            one += [up[chunk][step], down[chunk][step]]
        one.append(up[chunk][4] if chunk == 0 else down[chunk][4])
        chunks.append(one)
    return chunks


def per_device(queries, passages, lengths, target_shard, passage_slot):
    z, x, core = lax.axis_index("z"), lax.axis_index("x"), lax.axis_index("core")
    position = lax.broadcasted_iota(jnp.int32, (1, 64, 1), 1)
    own = jnp.where(position < lengths[:, None, None], passages, passages[:, :1]).reshape(4096, 128)
    swap = lambda value: lax.ppermute(value, "core", [(0, 1), (1, 0)])
    after = shift(own, "x", NX, 1)
    before = shift(own, "x", NX, -1)
    ahead = shift(queries, "group", 4, 1)
    behind = shift(queries, "group", 4, -1)
    across = shift(queries, "group", 4, 2)
    near = jnp.concatenate([queries, ahead], axis=1)
    far = jnp.concatenate([behind, across], axis=1)
    near, far = ring(near, far)
    third = shift(after[:2048], "x", NX, 1)
    fourth = shift(before[2048:], "x", NX, -1)

    targets = target_shard.reshape(256)
    onehot = (targets[:, None] == lax.broadcasted_iota(jnp.int32, (256, 64), 1))
    triangle = (lax.broadcasted_iota(jnp.int32, (256, 256), 0)
                > lax.broadcasted_iota(jnp.int32, (256, 256), 1)).astype(jnp.bfloat16)
    onehot_b = onehot.astype(jnp.bfloat16)
    earlier = jnp.dot(triangle, onehot_b, preferred_element_type=jnp.float32)
    rank = jnp.sum(jnp.where(onehot, earlier, 0.0), axis=1).astype(jnp.int32)
    lane = lax.broadcasted_iota(jnp.int32, (256, 128), 1)
    slots = jnp.tile(passage_slot.reshape(256, 16), (1, 8))
    number = lax.broadcasted_iota(jnp.int32, (256, 128), 0) // 8 + 1
    entry = jnp.where((lane < 96) & (lane // 16 == rank[:, None]), slots, 0)
    entry = jnp.where(lane == ROW_LANE + rank[:, None], number, entry)
    table = lax.dot_general(onehot_b, entry.astype(jnp.bfloat16), (((0,), (0,)), ((), ())),
                            preferred_element_type=jnp.float32).astype(jnp.int32)
    table = lax.all_to_all(table.reshape(8, 8, 128), "z", split_axis=0, concat_axis=0, tiled=True)

    distance = jnp.array([0, 1, -1, 2, -2, 3, -3, 4], jnp.int32)
    origin = jnp.mod(z - distance, NZ)
    step = jnp.array([0, 0, -1, -1, 1, 1, 2, 2], jnp.int32)
    other = jnp.array([0, 1, 0, 1, 0, 1, 0, 1], jnp.int32)
    block = jnp.mod(x + step, NX) * NC + jnp.bitwise_xor(core, other)
    ids = jnp.concatenate([origin, block])

    first = score([(i, (i,)) for i in range(6)], table, ids,
                  [own, swap(own), after, swap(after), before, swap(before)], near, far)
    second = score([(6, (0, 1))], table, ids, [third, fourth], near, far, first)
    last = score([(7, (0, 1))], table, ids, [swap(third), swap(fourth)], near, far, second)
    back = lax.all_to_all(last, "z", split_axis=0, concat_axis=0, tiled=True)
    flat = back[:, :, :96].reshape(64 * RANKS, 16)
    picked = flat[targets * RANKS + rank]
    return picked.reshape(1, 32, 8, 16)


def solution(mesh):
    fine = Mesh(mesh.devices.reshape(4, NZ, NX, NC), ("group", "z", "x", "core"))
    shard = ("z", "x", "core")
    in_specs = (
        P(shard, "group", None),
        P(("group",) + shard, None, None),
        P(("group",) + shard),
        P("group", shard, None),
        P("group", shard, None, None),
    )
    out_specs = P("group", shard, None, None)
    return jax.shard_map(per_device, mesh=fine, in_specs=in_specs, out_specs=out_specs, check_vma=False)
```

```python
import functools
import jax
import jax.numpy as jnp
from jax import lax
from jax.experimental import pallas as pl
from jax.experimental.pallas import tpu as pltpu
from jax.sharding import Mesh, PartitionSpec as P

NZ, NX, NC = 8, 4, 2
RANKS = 6
NT = (((1,), (1,)), ((), ()))
ROW_LANE = 96
CHUNK = 512


def score_kernel(first, sources, chained, *refs):
    many = len(sources)
    out, blocks, tokens, words, best, table_v, table_s, sems = refs[-8:]
    count = blocks.shape[0]
    ids = refs[0]
    inputs = refs[1:1 + count + many]
    copies = [pltpu.make_async_copy(inputs[count + s], tokens.at[s], sems.at[count + s]) for s in range(many)]
    copies += [pltpu.make_async_copy(inputs[b], blocks.at[b], sems.at[b]) for b in range(count)]
    for copy in copies:
        copy.start()
    if chained:
        out[...] = refs[1 + count + many][...]
    width = 32 * many
    lane = lax.broadcasted_iota(jnp.int32, (many, 128), 1)
    origin = [ids[s] for s in sources]
    for copy in copies[:many]:
        copy.wait()
    for s in range(many):
        mine = tokens[s, 64 + ids[16]].astype(jnp.float32)
        table_v[s] = mine[:8].astype(jnp.int32)
    scalars = pltpu.make_async_copy(table_v, table_s, sems.at[count + many])
    scalars.start()
    scalars.wait()

    def work(b, block, rows, ranks):
        for i in range(ranks):
            for s in range(many):
                row = jnp.maximum(rows[i][s] - 1, 0)
                start = i * width + s * 32
                words[start:start + 16, :] = tokens[s, 2 * row]
                words[start + 16:start + 32, :] = tokens[s, 2 * row + 1]
        stop = ranks * width
        held = words[:stop, :]
        for c in range(0, 4096, CHUNK):
            similar = lax.dot_general(blocks[b, c:c + CHUNK, :], held, NT, preferred_element_type=jnp.float32)
            best[c // 64:(c + CHUNK) // 64, :stop] = jnp.max(similar.reshape(CHUNK // 64, 64, stop), axis=1)
        value = best[:, :stop]
        picks = (ranks * many, stop)
        ones = (lax.broadcasted_iota(jnp.int32, picks, 1) // 32
                == lax.broadcasted_iota(jnp.int32, picks, 0)).astype(jnp.bfloat16)
        total = jnp.zeros((ranks * many, 64), jnp.float32)
        for _ in range(3):
            piece = value.astype(jnp.bfloat16)
            total += lax.dot_general(ones, piece, NT, preferred_element_type=jnp.float32)
            value = value - piece.astype(jnp.float32)
        total = total * jnp.float32(1.0 / 32)
        total = jnp.concatenate([total, total], axis=1)
        index = jnp.concatenate([table_v[s, pl.ds(block, 1), :] for s in range(many)], axis=0)
        index = jnp.bitwise_and(index, 63)
        result = jnp.zeros((many, 128), jnp.float32)
        for i in range(ranks):
            found = jnp.take_along_axis(total[i * many:(i + 1) * many], index, axis=1)
            result = jnp.where(lane // 16 == i, found, result)
        for s in range(many):
            out[origin[s], pl.ds(block, 1), :] = result[s:s + 1]

    @pl.loop(0, count)
    def _(b):
        for k in range(count):
            @pl.when(b == k)
            def _():
                copies[many + k].wait()
        block = ids[8 + first + b]
        rows = [[table_s[s, block, ROW_LANE + i] for s in range(many)]
                for i in range(RANKS)]
        used = [functools.reduce(lambda p, q: p + q, rows[i] + rows[i + 1]) > 0 for i in range(0, RANKS, 2)]

        @pl.when(used[2])
        def _():
            work(b, block, rows, 6)

        @pl.when(jnp.logical_and(used[1], jnp.logical_not(used[2])))
        def _():
            work(b, block, rows, 4)

        @pl.when(jnp.logical_and(used[0], jnp.logical_not(used[1])))
        def _():
            work(b, block, rows, 2)


def score(first, sources, ids, passages, tokens, previous=None, cost=1):
    smem = pl.BlockSpec(memory_space=pltpu.SMEM)
    vmem = pl.BlockSpec(memory_space=pltpu.VMEM)
    held = pl.BlockSpec(memory_space=pl.ANY)
    many, count = len(sources), len(passages)
    operands = [ids, *passages, *tokens]
    specs = [smem] + [held] * (len(operands) - 1)
    if previous is not None:
        operands.append(previous)
        specs.append(vmem)
    live = count * 4096 * 32 * many * RANKS
    return pl.pallas_call(
        functools.partial(score_kernel, first, sources, previous is not None),
        in_specs=specs,
        out_specs=vmem,
        out_shape=jax.ShapeDtypeStruct((8, 8, 128), jnp.float32),
        scratch_shapes=[
            pltpu.VMEM((count, 4096, 128), jnp.bfloat16),
            pltpu.VMEM((many, 72, 16, 128), jnp.bfloat16),
            pltpu.VMEM((RANKS * 32 * many, 128), jnp.bfloat16),
            pltpu.VMEM((64, RANKS * 32 * many), jnp.float32),
            pltpu.VMEM((many, 8, 128), jnp.int32),
            pltpu.SMEM((many, 8, 128), jnp.int32),
            pltpu.SemaphoreType.DMA((count + many + 1,)),
        ],
        compiler_params=pltpu.CompilerParams(vmem_limit_bytes=16 * 2**20),
        cost_estimate=pl.CostEstimate(flops=cost * 128 * live, bytes_accessed=2**20, transcendentals=0),
    )(*operands)


def fill_kernel(lengths, passages, out):
    position = lax.broadcasted_iota(jnp.int32, (64, 128), 0)
    for j in range(64):
        value = passages[j].astype(jnp.float32)
        value = jnp.where(position < lengths[j], value, value[:1])
        out[j * 64:(j + 1) * 64, :] = value.astype(jnp.bfloat16)


def fill(lengths, passages):
    return pl.pallas_call(
        fill_kernel,
        in_specs=[pl.BlockSpec(memory_space=pltpu.SMEM), pl.BlockSpec(memory_space=pltpu.VMEM)],
        out_specs=pl.BlockSpec(memory_space=pltpu.VMEM),
        out_shape=jax.ShapeDtypeStruct((4096, 128), jnp.bfloat16),
        cost_estimate=pl.CostEstimate(flops=2**20, bytes_accessed=2**21, transcendentals=0),
    )(lengths, passages)


def shift(value, axis, size, by):
    return lax.ppermute(value, axis, [(i, (i + by) % size) for i in range(size)])


def per_device(queries, passages, lengths, target_shard, passage_slot):
    z, x, core = lax.axis_index("z"), lax.axis_index("x"), lax.axis_index("core")
    ahead = shift(queries, "group", 4, 1)
    behind = shift(queries, "group", 4, -1)
    across = shift(queries, "group", 4, 2)
    own = fill(lengths, passages)
    swap = lambda value: lax.ppermute(value, "core", [(0, 1), (1, 0)])
    after = shift(own, "x", NX, 1)
    before = shift(own, "x", NX, -1)
    targets = target_shard.reshape(256)
    onehot = (targets[:, None] == lax.broadcasted_iota(jnp.int32, (256, 64), 1))
    triangle = (lax.broadcasted_iota(jnp.int32, (256, 256), 0)
                > lax.broadcasted_iota(jnp.int32, (256, 256), 1)).astype(jnp.bfloat16)
    onehot_b = onehot.astype(jnp.bfloat16)
    earlier = jnp.dot(triangle, onehot_b, preferred_element_type=jnp.float32)
    rank = jnp.sum(jnp.where(onehot, earlier, 0.0), axis=1).astype(jnp.int32)
    lane = lax.broadcasted_iota(jnp.int32, (256, 128), 1)
    slots = jnp.tile(passage_slot.reshape(256, 16), (1, 8))
    number = lax.broadcasted_iota(jnp.int32, (256, 128), 0) // 8 + 1
    entry = jnp.where((lane < 96) & (lane // 16 == rank[:, None]), slots, 0)
    entry = jnp.where(lane == ROW_LANE + rank[:, None], number, entry)
    table = lax.dot_general(onehot_b, entry.astype(jnp.bfloat16), (((0,), (0,)), ((), ())),
                            preferred_element_type=jnp.float32).astype(jnp.bfloat16)
    table = jnp.pad(table.reshape(8, 8, 128), ((0, 0), (0, 8), (0, 0)))
    whole = jnp.concatenate([queries, ahead, behind, across], axis=1).reshape(64, 16, 128)
    whole = jnp.concatenate([whole, table], axis=0)
    home = swap(own)
    whole, home = lax.optimization_barrier((whole, home))

    up1 = shift(whole, "z", NZ, 1)
    down1 = shift(whole, "z", NZ, -1)
    up2 = shift(whole, "z", NZ, 2)
    up1, whole = lax.optimization_barrier((up1, whole))
    down2 = shift(whole, "z", NZ, -2)

    distance = jnp.array([0, 1, -1, 2, -2, 3, -3, 4], jnp.int32)
    origin = jnp.mod(z - distance, NZ)
    step = jnp.array([0, 0, -1, -1, 1, 1, 2, 2], jnp.int32)
    other = jnp.array([0, 1, 0, 1, 0, 1, 0, 1], jnp.int32)
    block = jnp.mod(x + step, NX) * NC + jnp.bitwise_xor(core, other)
    ids = jnp.concatenate([origin, block, z[None]])

    early, late = (0, 1, 2, 3), (4, 5, 6, 7)
    out = score(0, early, ids, [own, home], [whole, up1, down1, up2], cost=0)
    up2, down2, after, before, out = lax.optimization_barrier((up2, down2, after, before, out))
    after_other = swap(after)
    before_other = swap(before)
    opposite = shift(after, "x", NX, 1)
    up3 = shift(up2, "z", NZ, 1)
    down3 = shift(down2, "z", NZ, -1)
    tokens = [whole, up1, down1, up2, down2]
    out = score(2, early, ids, [after, after_other], tokens[:4], out)
    before_other, up3, out = lax.optimization_barrier((before_other, up3, out))
    up4 = shift(up3, "z", NZ, 1)
    out = score(4, early, ids, [before, before_other], tokens[:4], out)
    up4, down3, out = lax.optimization_barrier((up4, down3, out))
    tokens = tokens + [up3, down3, up4]
    out = score(0, late, ids, [own, home, after, after_other, before, before_other], tokens[4:], out)
    opposite, out = lax.optimization_barrier((opposite, out))
    facing = swap(opposite)
    out = score(6, early + late, ids, [opposite], tokens, out)
    last = score(7, early + late, ids, [facing], tokens, out)
    back = lax.all_to_all(last, "z", split_axis=0, concat_axis=0, tiled=True)
    flat = back[:, :, :96].reshape(64 * RANKS, 16)
    picked = flat[targets * RANKS + rank]
    return picked.reshape(1, 32, 8, 16)


def solution(mesh):
    fine = Mesh(mesh.devices.reshape(4, NZ, NX, NC), ("group", "z", "x", "core"))
    shard = ("z", "x", "core")
    in_specs = (
        P(shard, "group", None),
        P(("group",) + shard, None, None),
        P(("group",) + shard),
        P("group", shard, None),
        P("group", shard, None, None),
    )
    out_specs = P("group", shard, None, None)
    return jax.shard_map(per_device, mesh=fine, in_specs=in_specs, out_specs=out_specs, check_vma=False)
```

```python
import functools
import jax
import jax.numpy as jnp
from jax import lax
from jax.experimental import pallas as pl
from jax.experimental.pallas import tpu as pltpu
from jax.sharding import Mesh, PartitionSpec as P

NZ, NX, NC = 8, 4, 2
RANKS = 6
NT = (((1,), (1,)), ((), ()))
ROW_LANE = 96
CHUNK = 512


def score_kernel(first, sources, chained, *refs):
    many = len(sources)
    out, blocks, tokens, words, best, table_v, table_s, sems = refs[-8:]
    count = blocks.shape[0]
    ids = refs[0]
    inputs = refs[1:1 + count + many]
    copies = [pltpu.make_async_copy(inputs[count + s], tokens.at[s], sems.at[count + s]) for s in range(many)]
    copies += [pltpu.make_async_copy(inputs[b], blocks.at[b], sems.at[b]) for b in range(count)]
    for copy in copies:
        copy.start()
    if chained:
        out[...] = refs[1 + count + many][...]
    width = 32 * many
    lane = lax.broadcasted_iota(jnp.int32, (many, 128), 1)
    origin = [ids[s] for s in sources]
    for copy in copies[:many]:
        copy.wait()
    for s in range(many):
        mine = tokens[s, 64 + ids[16]].astype(jnp.float32)
        table_v[s] = mine[:8].astype(jnp.int32)
    scalars = pltpu.make_async_copy(table_v, table_s, sems.at[count + many])
    scalars.start()
    scalars.wait()

    def work(b, block, rows, ranks):
        for i in range(ranks):
            for s in range(many):
                row = jnp.maximum(rows[i][s] - 1, 0)
                start = i * width + s * 32
                words[start:start + 16, :] = tokens[s, 2 * row]
                words[start + 16:start + 32, :] = tokens[s, 2 * row + 1]
        stop = ranks * width
        held = words[:stop, :]
        for c in range(0, 4096, CHUNK):
            similar = lax.dot_general(blocks[b, c:c + CHUNK, :], held, NT, preferred_element_type=jnp.float32)
            best[c // 64:(c + CHUNK) // 64, :stop] = jnp.max(similar.reshape(CHUNK // 64, 64, stop), axis=1)
        value = best[:, :stop]
        picks = (ranks * many, stop)
        ones = (lax.broadcasted_iota(jnp.int32, picks, 1) // 32
                == lax.broadcasted_iota(jnp.int32, picks, 0)).astype(jnp.bfloat16)
        total = jnp.zeros((ranks * many, 64), jnp.float32)
        for _ in range(3):
            piece = value.astype(jnp.bfloat16)
            total += lax.dot_general(ones, piece, NT, preferred_element_type=jnp.float32)
            value = value - piece.astype(jnp.float32)
        total = total * jnp.float32(1.0 / 32)
        total = jnp.concatenate([total, total], axis=1)
        index = jnp.concatenate([table_v[s, pl.ds(block, 1), :] for s in range(many)], axis=0)
        index = jnp.bitwise_and(index, 63)
        result = jnp.zeros((many, 128), jnp.float32)
        for i in range(ranks):
            found = jnp.take_along_axis(total[i * many:(i + 1) * many], index, axis=1)
            result = jnp.where(lane // 16 == i, found, result)
        for s in range(many):
            out[origin[s], pl.ds(block, 1), :] = result[s:s + 1]

    @pl.loop(0, count)
    def _(b):
        for k in range(count):
            @pl.when(b == k)
            def _():
                copies[many + k].wait()
        block = ids[8 + first + b]
        rows = [[table_s[s, block, ROW_LANE + i] for s in range(many)]
                for i in range(RANKS)]
        used = [functools.reduce(lambda p, q: p + q, rows[i] + rows[i + 1]) > 0 for i in range(0, RANKS, 2)]

        @pl.when(used[2])
        def _():
            work(b, block, rows, 6)

        @pl.when(jnp.logical_and(used[1], jnp.logical_not(used[2])))
        def _():
            work(b, block, rows, 4)

        @pl.when(jnp.logical_and(used[0], jnp.logical_not(used[1])))
        def _():
            work(b, block, rows, 2)


def score(first, sources, ids, passages, tokens, previous=None, cost=1):
    smem = pl.BlockSpec(memory_space=pltpu.SMEM)
    vmem = pl.BlockSpec(memory_space=pltpu.VMEM)
    held = pl.BlockSpec(memory_space=pl.ANY)
    many, count = len(sources), len(passages)
    operands = [ids, *passages, *tokens]
    specs = [smem] + [held] * (len(operands) - 1)
    if first == 0:
        specs[1] = specs[2] = pl.BlockSpec(memory_space=pltpu.HBM)
    if previous is not None:
        operands.append(previous)
        specs.append(vmem)
    live = count * 4096 * 32 * many * RANKS
    return pl.pallas_call(
        functools.partial(score_kernel, first, sources, previous is not None),
        in_specs=specs,
        out_specs=vmem,
        out_shape=jax.ShapeDtypeStruct((8, 8, 128), jnp.float32),
        scratch_shapes=[
            pltpu.VMEM((count, 4096, 128), jnp.bfloat16),
            pltpu.VMEM((many, 72, 16, 128), jnp.bfloat16),
            pltpu.VMEM((RANKS * 32 * many, 128), jnp.bfloat16),
            pltpu.VMEM((64, RANKS * 32 * many), jnp.float32),
            pltpu.VMEM((many, 8, 128), jnp.int32),
            pltpu.SMEM((many, 8, 128), jnp.int32),
            pltpu.SemaphoreType.DMA((count + many + 1,)),
        ],
        compiler_params=pltpu.CompilerParams(vmem_limit_bytes=16 * 2**20),
        cost_estimate=pl.CostEstimate(flops=cost * 128 * live, bytes_accessed=2**20, transcendentals=0),
    )(*operands)


def fill_kernel(lengths, passages, out):
    position = lax.broadcasted_iota(jnp.int32, (64, 128), 0)
    for j in range(64):
        value = passages[j].astype(jnp.float32)
        value = jnp.where(position < lengths[j], value, value[:1])
        out[j * 64:(j + 1) * 64, :] = value.astype(jnp.bfloat16)


def fill(lengths, passages):
    return pl.pallas_call(
        fill_kernel,
        in_specs=[pl.BlockSpec(memory_space=pltpu.SMEM), pl.BlockSpec(memory_space=pltpu.VMEM)],
        out_specs=pl.BlockSpec(memory_space=pltpu.VMEM),
        out_shape=jax.ShapeDtypeStruct((4096, 128), jnp.bfloat16),
        cost_estimate=pl.CostEstimate(flops=2**20, bytes_accessed=2**21, transcendentals=0),
    )(lengths, passages)


def shift(value, axis, size, by):
    return lax.ppermute(value, axis, [(i, (i + by) % size) for i in range(size)])


def per_device(queries, passages, lengths, target_shard, passage_slot):
    z, x, core = lax.axis_index("z"), lax.axis_index("x"), lax.axis_index("core")
    pair = lax.ppermute(queries, "group", [(0, 1), (1, 0), (2, 3), (3, 2)])
    own = fill(lengths, passages)
    swap = lambda value: lax.ppermute(value, "core", [(0, 1), (1, 0)])
    pair, own = lax.optimization_barrier((pair, own))
    home = swap(own)
    after = shift(own, "x", NX, 1)
    before = shift(own, "x", NX, -1)

    targets = target_shard.reshape(256)
    onehot = (targets[:, None] == lax.broadcasted_iota(jnp.int32, (256, 64), 1))
    triangle = (lax.broadcasted_iota(jnp.int32, (256, 256), 0)
                > lax.broadcasted_iota(jnp.int32, (256, 256), 1)).astype(jnp.bfloat16)
    onehot_b = onehot.astype(jnp.bfloat16)
    earlier = jnp.dot(triangle, onehot_b, preferred_element_type=jnp.float32)
    rank = jnp.sum(jnp.where(onehot, earlier, 0.0), axis=1).astype(jnp.int32)
    lane = lax.broadcasted_iota(jnp.int32, (256, 128), 1)
    slots = jnp.tile(passage_slot.reshape(256, 16), (1, 8))
    number = lax.broadcasted_iota(jnp.int32, (256, 128), 0) // 8 + 1
    entry = jnp.where((lane < 96) & (lane // 16 == rank[:, None]), slots, 0)
    entry = jnp.where(lane == ROW_LANE + rank[:, None], number, entry)
    table = lax.dot_general(onehot_b, entry.astype(jnp.bfloat16), (((0,), (0,)), ((), ())),
                            preferred_element_type=jnp.float32).astype(jnp.bfloat16)
    table = jnp.pad(table.reshape(8, 8, 128), ((0, 0), (0, 8), (0, 0)))
    pair = jnp.concatenate([queries, pair], axis=1)
    rest = lax.ppermute(pair, "group", [(0, 3), (3, 0), (1, 2), (2, 1)])
    whole = jnp.concatenate([pair, rest], axis=1).reshape(64, 16, 128)
    whole = jnp.concatenate([whole, table], axis=0)
    whole, home = lax.optimization_barrier((whole, home))

    up1 = shift(whole, "z", NZ, 1)
    down1 = shift(whole, "z", NZ, -1)
    up2 = shift(up1, "z", NZ, 1)
    down2 = shift(down1, "z", NZ, -1)

    distance = jnp.array([0, 1, -1, 2, -2, 3, -3, 4], jnp.int32)
    origin = jnp.mod(z - distance, NZ)
    step = jnp.array([0, 0, -1, 1, -1, 1, 2, 2], jnp.int32)
    other = jnp.array([1, 0, 0, 0, 1, 1, 0, 1], jnp.int32)
    block = jnp.mod(x + step, NX) * NC + jnp.bitwise_xor(core, other)
    ids = jnp.concatenate([origin, block, z[None]])

    early, late = (0, 1, 2, 3), (4, 5, 6, 7)
    out = score(0, early, ids, [home, own], [whole, up1, down1, up2], cost=0)
    up3 = shift(up2, "z", NZ, 1)
    down3 = shift(down2, "z", NZ, -1)
    up3, down3, after, before, out = lax.optimization_barrier((up3, down3, after, before, out))
    after_other = swap(after)
    before_other = swap(before)
    up4 = shift(up3, "z", NZ, 1)
    opposite = shift(after, "x", NX, 1)
    tokens = [whole, up1, down1, up2, down2]
    out = score(2, early, ids, [after, before, after_other, before_other], tokens[:4], out)
    up4, out = lax.optimization_barrier((up4, out))
    tokens = tokens + [up3, down3, up4]
    out = score(0, late, ids, [home, own, after, before, after_other, before_other], tokens[4:], out)
    opposite, out = lax.optimization_barrier((opposite, out))
    facing = swap(opposite)
    out = score(6, early + late, ids, [opposite], tokens, out)
    last = score(7, early + late, ids, [facing], tokens, out)
    back = lax.all_to_all(last, "z", split_axis=0, concat_axis=0, tiled=True)
    flat = back[:, :, :96].reshape(64 * RANKS, 16)
    picked = flat[targets * RANKS + rank]
    return picked.reshape(1, 32, 8, 16)


def solution(mesh):
    fine = Mesh(mesh.devices.reshape(4, NZ, NX, NC), ("group", "z", "x", "core"))
    shard = ("z", "x", "core")
    in_specs = (
        P(shard, "group", None),
        P(("group",) + shard, None, None),
        P(("group",) + shard),
        P("group", shard, None),
        P("group", shard, None, None),
    )
    out_specs = P("group", shard, None, None)
    return jax.shard_map(per_device, mesh=fine, in_specs=in_specs, out_specs=out_specs, check_vma=False)
```

```python
import functools
import jax
import jax.numpy as jnp
from jax import lax
from jax.experimental import pallas as pl
from jax.experimental.pallas import tpu as pltpu
from jax.sharding import Mesh, PartitionSpec as P

NZ, NX, NC = 8, 4, 2
RANKS = 6
NT = (((1,), (1,)), ((), ()))
ROW_LANE = 96
CHUNK = 512


def score_kernel(first, sources, chained, *refs):
    many = len(sources)
    out, blocks, words, best, table_v, table_s, sems = refs[-7:]
    count = blocks.shape[0]
    ids = refs[0]
    inputs = refs[1:1 + count]
    tokens = refs[1 + count:1 + count + many]
    copies = [pltpu.make_async_copy(inputs[b], blocks.at[b], sems.at[b]) for b in range(count)]
    for copy in copies:
        copy.start()
    if chained:
        out[...] = refs[1 + count + many][...]
    width = 32 * many
    lane = lax.broadcasted_iota(jnp.int32, (many, 128), 1)
    origin = [ids[s] for s in sources]
    for s in range(many):
        mine = tokens[s][64 + ids[16]].astype(jnp.float32)
        table_v[s] = mine[:8].astype(jnp.int32)
    scalars = pltpu.make_async_copy(table_v, table_s, sems.at[count])
    scalars.start()
    scalars.wait()

    def work(b, block, rows, ranks):
        for i in range(ranks):
            for s in range(many):
                row = jnp.maximum(rows[i][s] - 1, 0)
                start = i * width + s * 32
                words[start:start + 16, :] = tokens[s][2 * row]
                words[start + 16:start + 32, :] = tokens[s][2 * row + 1]
        stop = ranks * width
        held = words[:stop, :]
        for c in range(0, 4096, CHUNK):
            similar = lax.dot_general(blocks[b, c:c + CHUNK, :], held, NT, preferred_element_type=jnp.float32)
            best[c // 64:(c + CHUNK) // 64, :stop] = jnp.max(similar.reshape(CHUNK // 64, 64, stop), axis=1)
        value = best[:, :stop]
        picks = (ranks * many, stop)
        ones = (lax.broadcasted_iota(jnp.int32, picks, 1) // 32
                == lax.broadcasted_iota(jnp.int32, picks, 0)).astype(jnp.bfloat16)
        total = jnp.zeros((ranks * many, 64), jnp.float32)
        for _ in range(3):
            piece = value.astype(jnp.bfloat16)
            total += lax.dot_general(ones, piece, NT, preferred_element_type=jnp.float32)
            value = value - piece.astype(jnp.float32)
        total = total * jnp.float32(1.0 / 32)
        total = jnp.concatenate([total, total], axis=1)
        index = jnp.concatenate([table_v[s, pl.ds(block, 1), :] for s in range(many)], axis=0)
        index = jnp.bitwise_and(index, 63)
        result = jnp.zeros((many, 128), jnp.float32)
        for i in range(ranks):
            found = jnp.take_along_axis(total[i * many:(i + 1) * many], index, axis=1)
            result = jnp.where(lane // 16 == i, found, result)
        for s in range(many):
            out[origin[s], pl.ds(block, 1), :] = result[s:s + 1]

    @pl.loop(0, count)
    def _(b):
        for k in range(count):
            @pl.when(b == k)
            def _():
                copies[k].wait()
        block = ids[8 + first + b]
        rows = [[table_s[s, block, ROW_LANE + i] for s in range(many)]
                for i in range(RANKS)]
        used = [functools.reduce(lambda p, q: p + q, rows[i] + rows[i + 1]) > 0 for i in range(0, RANKS, 2)]

        @pl.when(used[2])
        def _():
            work(b, block, rows, 6)

        @pl.when(jnp.logical_and(used[1], jnp.logical_not(used[2])))
        def _():
            work(b, block, rows, 4)

        @pl.when(jnp.logical_and(used[0], jnp.logical_not(used[1])))
        def _():
            work(b, block, rows, 2)


def score(first, sources, ids, passages, tokens, previous=None, cost=1):
    smem = pl.BlockSpec(memory_space=pltpu.SMEM)
    vmem = pl.BlockSpec(memory_space=pltpu.VMEM)
    held = pl.BlockSpec(memory_space=pl.ANY)
    many, count = len(sources), len(passages)
    operands = [ids, *passages, *tokens]
    specs = [smem] + [held] * count + [vmem] * many
    if previous is not None:
        operands.append(previous)
        specs.append(vmem)
    live = count * 4096 * 32 * many * RANKS
    return pl.pallas_call(
        functools.partial(score_kernel, first, sources, previous is not None),
        in_specs=specs,
        out_specs=vmem,
        out_shape=jax.ShapeDtypeStruct((8, 8, 128), jnp.float32),
        scratch_shapes=[
            pltpu.VMEM((count, 4096, 128), jnp.bfloat16),
            pltpu.VMEM((RANKS * 32 * many, 128), jnp.bfloat16),
            pltpu.VMEM((64, RANKS * 32 * many), jnp.float32),
            pltpu.VMEM((many, 8, 128), jnp.int32),
            pltpu.SMEM((many, 8, 128), jnp.int32),
            pltpu.SemaphoreType.DMA((count + 1,)),
        ],
        compiler_params=pltpu.CompilerParams(vmem_limit_bytes=16 * 2**20),
        cost_estimate=pl.CostEstimate(flops=cost * 128 * live, bytes_accessed=2**20, transcendentals=0),
    )(*operands)


def fill_kernel(lengths, passages, out):
    position = lax.broadcasted_iota(jnp.int32, (64, 128), 0)
    for j in range(64):
        value = passages[j].astype(jnp.float32)
        value = jnp.where(position < lengths[j], value, value[:1])
        out[j * 64:(j + 1) * 64, :] = value.astype(jnp.bfloat16)


def fill(lengths, passages):
    return pl.pallas_call(
        fill_kernel,
        in_specs=[pl.BlockSpec(memory_space=pltpu.SMEM), pl.BlockSpec(memory_space=pltpu.VMEM)],
        out_specs=pl.BlockSpec(memory_space=pltpu.VMEM),
        out_shape=jax.ShapeDtypeStruct((4096, 128), jnp.bfloat16),
        cost_estimate=pl.CostEstimate(flops=2**20, bytes_accessed=2**21, transcendentals=0),
    )(lengths, passages)


def shift(value, axis, size, by):
    return lax.ppermute(value, axis, [(i, (i + by) % size) for i in range(size)])


def per_device(queries, passages, lengths, target_shard, passage_slot):
    z, x, core = lax.axis_index("z"), lax.axis_index("x"), lax.axis_index("core")
    pair = lax.ppermute(queries, "group", [(0, 1), (1, 0), (2, 3), (3, 2)])
    own = fill(lengths, passages)
    swap = lambda value: lax.ppermute(value, "core", [(0, 1), (1, 0)])
    pair, own = lax.optimization_barrier((pair, own))
    home = swap(own)
    after = shift(own, "x", NX, 1)
    before = shift(own, "x", NX, -1)

    targets = target_shard.reshape(256)
    onehot = (targets[:, None] == lax.broadcasted_iota(jnp.int32, (256, 64), 1))
    triangle = (lax.broadcasted_iota(jnp.int32, (256, 256), 0)
                > lax.broadcasted_iota(jnp.int32, (256, 256), 1)).astype(jnp.bfloat16)
    onehot_b = onehot.astype(jnp.bfloat16)
    earlier = jnp.dot(triangle, onehot_b, preferred_element_type=jnp.float32)
    rank = jnp.sum(jnp.where(onehot, earlier, 0.0), axis=1).astype(jnp.int32)
    lane = lax.broadcasted_iota(jnp.int32, (256, 128), 1)
    slots = jnp.tile(passage_slot.reshape(256, 16), (1, 8))
    number = lax.broadcasted_iota(jnp.int32, (256, 128), 0) // 8 + 1
    entry = jnp.where((lane < 96) & (lane // 16 == rank[:, None]), slots, 0)
    entry = jnp.where(lane == ROW_LANE + rank[:, None], number, entry)
    table = lax.dot_general(onehot_b, entry.astype(jnp.bfloat16), (((0,), (0,)), ((), ())),
                            preferred_element_type=jnp.float32).astype(jnp.bfloat16)
    table = jnp.pad(table.reshape(8, 8, 128), ((0, 0), (0, 8), (0, 0)))
    pair = jnp.concatenate([queries, pair], axis=1)
    rest = lax.ppermute(pair, "group", [(0, 3), (3, 0), (1, 2), (2, 1)])
    whole = jnp.concatenate([pair, rest], axis=1).reshape(64, 16, 128)
    whole = jnp.concatenate([whole, table], axis=0)
    whole, _ = lax.optimization_barrier((whole, home[:16]))

    up1 = shift(whole, "z", NZ, 1)
    down1 = shift(whole, "z", NZ, -1)
    up2 = shift(up1, "z", NZ, 1)
    down2 = shift(down1, "z", NZ, -1)

    distance = jnp.array([0, 1, -1, 2, -2, 3, -3, 4], jnp.int32)
    origin = jnp.mod(z - distance, NZ)
    step = jnp.array([0, 0, -1, 1, -1, 1, 2, 2], jnp.int32)
    other = jnp.array([1, 0, 0, 0, 1, 1, 0, 1], jnp.int32)
    block = jnp.mod(x + step, NX) * NC + jnp.bitwise_xor(core, other)
    ids = jnp.concatenate([origin, block, z[None]])

    early, late = (0, 1, 2, 3), (4, 5, 6, 7)
    out = score(0, early, ids, [home, own], [whole, up1, down1, up2], cost=0)
    up3 = shift(up2, "z", NZ, 1)
    down3 = shift(down2, "z", NZ, -1)
    up3, down3, after, before, out = lax.optimization_barrier((up3, down3, after, before, out))
    after_other = swap(after)
    before_other = swap(before)
    up4 = shift(up3, "z", NZ, 1)
    opposite = shift(after, "x", NX, 1)
    tokens = [whole, up1, down1, up2, down2]
    out = score(2, early, ids, [after, before, after_other, before_other], tokens[:4], out)
    up4, out = lax.optimization_barrier((up4, out))
    tokens = tokens + [up3, down3, up4]
    out = score(0, late, ids, [home, own, after, before, after_other, before_other], tokens[4:], out)
    opposite, out = lax.optimization_barrier((opposite, out))
    facing = swap(opposite)
    out = score(6, early + late, ids, [opposite], tokens, out)
    last = score(7, early + late, ids, [facing], tokens, out)
    back = lax.all_to_all(last, "z", split_axis=0, concat_axis=0, tiled=True)
    flat = back[:, :, :96].reshape(64 * RANKS, 16)
    picked = flat[targets * RANKS + rank]
    return picked.reshape(1, 32, 8, 16)


def solution(mesh):
    fine = Mesh(mesh.devices.reshape(4, NZ, NX, NC), ("group", "z", "x", "core"))
    shard = ("z", "x", "core")
    in_specs = (
        P(shard, "group", None),
        P(("group",) + shard, None, None),
        P(("group",) + shard),
        P("group", shard, None),
        P("group", shard, None, None),
    )
    out_specs = P("group", shard, None, None)
    return jax.shard_map(per_device, mesh=fine, in_specs=in_specs, out_specs=out_specs, check_vma=False)
```

```python
import functools
import jax
import jax.numpy as jnp
from jax import lax
from jax.experimental import pallas as pl
from jax.experimental.pallas import tpu as pltpu
from jax.sharding import Mesh, PartitionSpec as P

NZ, NX, NC = 8, 4, 2
RANKS = 6
NT = (((1,), (1,)), ((), ()))
ROW_LANE = 96
CHUNK = 1024


def score_kernel(first, sources, chained, *refs):
    many = len(sources)
    out, blocks, words, best, table_v, table_s, sems = refs[-7:]
    count = blocks.shape[0]
    ids = refs[0]
    inputs = refs[1:1 + count]
    tokens = refs[1 + count:1 + count + many]
    copies = [pltpu.make_async_copy(inputs[b], blocks.at[b], sems.at[b]) for b in range(count)]
    for copy in copies:
        copy.start()
    if chained:
        out[...] = refs[1 + count + many][...]
    width = 32 * many
    lane = lax.broadcasted_iota(jnp.int32, (many, 128), 1)
    origin = [ids[s] for s in sources]
    for s in range(many):
        mine = tokens[s][64 + ids[16]].astype(jnp.float32)
        table_v[s] = mine[:8].astype(jnp.int32)
    scalars = pltpu.make_async_copy(table_v, table_s, sems.at[count])
    scalars.start()
    scalars.wait()

    def work(b, block, rows, ranks):
        for i in range(ranks):
            for s in range(many):
                row = jnp.maximum(rows[i][s] - 1, 0)
                start = i * width + s * 32
                words[start:start + 16, :] = tokens[s][2 * row]
                words[start + 16:start + 32, :] = tokens[s][2 * row + 1]
        stop = ranks * width
        held = words[:stop, :]
        for c in range(0, 4096, CHUNK):
            similar = lax.dot_general(blocks[b, c:c + CHUNK, :], held, NT, preferred_element_type=jnp.float32)
            best[c // 64:(c + CHUNK) // 64, :stop] = jnp.max(similar.reshape(CHUNK // 64, 64, stop), axis=1)
        value = best[:, :stop]
        picks = (ranks * many, stop)
        ones = (lax.broadcasted_iota(jnp.int32, picks, 1) // 32
                == lax.broadcasted_iota(jnp.int32, picks, 0)).astype(jnp.bfloat16)
        total = jnp.zeros((ranks * many, 64), jnp.float32)
        for _ in range(2):
            piece = value.astype(jnp.bfloat16)
            total += lax.dot_general(ones, piece, NT, preferred_element_type=jnp.float32)
            value = value - piece.astype(jnp.float32)
        total = total * jnp.float32(1.0 / 32)
        total = jnp.concatenate([total, total], axis=1)
        index = jnp.concatenate([table_v[s, pl.ds(block, 1), :] for s in range(many)], axis=0)
        index = jnp.bitwise_and(index, 63)
        result = jnp.zeros((many, 128), jnp.float32)
        for i in range(ranks):
            found = jnp.take_along_axis(total[i * many:(i + 1) * many], index, axis=1)
            result = jnp.where(lane // 16 == i, found, result)
        for s in range(many):
            out[origin[s], pl.ds(block, 1), :] = result[s:s + 1]

    @pl.loop(0, count)
    def _(b):
        for k in range(count):
            @pl.when(b == k)
            def _():
                copies[k].wait()
        block = ids[8 + first + b]
        rows = [[table_s[s, block, ROW_LANE + i] for s in range(many)]
                for i in range(RANKS)]
        used = [functools.reduce(lambda p, q: p + q, rows[i] + rows[i + 1]) > 0 for i in range(0, RANKS, 2)]

        @pl.when(used[2])
        def _():
            work(b, block, rows, 6)

        @pl.when(jnp.logical_and(used[1], jnp.logical_not(used[2])))
        def _():
            work(b, block, rows, 4)

        @pl.when(jnp.logical_and(used[0], jnp.logical_not(used[1])))
        def _():
            work(b, block, rows, 2)


def score(first, sources, ids, passages, tokens, previous=None, cost=1):
    smem = pl.BlockSpec(memory_space=pltpu.SMEM)
    vmem = pl.BlockSpec(memory_space=pltpu.VMEM)
    held = pl.BlockSpec(memory_space=pl.ANY)
    many, count = len(sources), len(passages)
    operands = [ids, *passages, *tokens]
    specs = [smem] + [held] * count + [vmem] * many
    if previous is not None:
        operands.append(previous)
        specs.append(vmem)
    live = count * 4096 * 32 * many * RANKS
    return pl.pallas_call(
        functools.partial(score_kernel, first, sources, previous is not None),
        in_specs=specs,
        out_specs=vmem,
        out_shape=jax.ShapeDtypeStruct((8, 8, 128), jnp.float32),
        scratch_shapes=[
            pltpu.VMEM((count, 4096, 128), jnp.bfloat16),
            pltpu.VMEM((RANKS * 32 * many, 128), jnp.bfloat16),
            pltpu.VMEM((64, RANKS * 32 * many), jnp.float32),
            pltpu.VMEM((many, 8, 128), jnp.int32),
            pltpu.SMEM((many, 8, 128), jnp.int32),
            pltpu.SemaphoreType.DMA((count + 1,)),
        ],
        compiler_params=pltpu.CompilerParams(vmem_limit_bytes=16 * 2**20),
        cost_estimate=pl.CostEstimate(flops=cost * 128 * live, bytes_accessed=2**20, transcendentals=0),
    )(*operands)


def fill_kernel(lengths, passages, out):
    position = lax.broadcasted_iota(jnp.int32, (64, 128), 0)
    for j in range(64):
        value = passages[j].astype(jnp.float32)
        value = jnp.where(position < lengths[j], value, value[:1])
        out[j * 64:(j + 1) * 64, :] = value.astype(jnp.bfloat16)


def fill(lengths, passages):
    return pl.pallas_call(
        fill_kernel,
        in_specs=[pl.BlockSpec(memory_space=pltpu.SMEM), pl.BlockSpec(memory_space=pltpu.VMEM)],
        out_specs=pl.BlockSpec(memory_space=pltpu.VMEM),
        out_shape=jax.ShapeDtypeStruct((4096, 128), jnp.bfloat16),
        cost_estimate=pl.CostEstimate(flops=2**20, bytes_accessed=2**21, transcendentals=0),
    )(lengths, passages)


def shift(value, axis, size, by):
    return lax.ppermute(value, axis, [(i, (i + by) % size) for i in range(size)])


def per_device(queries, passages, lengths, target_shard, passage_slot):
    z, x, core = lax.axis_index("z"), lax.axis_index("x"), lax.axis_index("core")
    pair = lax.ppermute(queries, "group", [(0, 1), (1, 0), (2, 3), (3, 2)])
    own = fill(lengths, passages)
    swap = lambda value: lax.ppermute(value, "core", [(0, 1), (1, 0)])
    pair, own = lax.optimization_barrier((pair, own))
    home = swap(own)
    after = shift(own, "x", NX, 1)
    before = shift(own, "x", NX, -1)

    targets = target_shard.reshape(256)
    onehot = (targets[:, None] == lax.broadcasted_iota(jnp.int32, (256, 64), 1))
    triangle = (lax.broadcasted_iota(jnp.int32, (256, 256), 0)
                > lax.broadcasted_iota(jnp.int32, (256, 256), 1)).astype(jnp.bfloat16)
    onehot_b = onehot.astype(jnp.bfloat16)
    earlier = jnp.dot(triangle, onehot_b, preferred_element_type=jnp.float32)
    rank = jnp.sum(jnp.where(onehot, earlier, 0.0), axis=1).astype(jnp.int32)
    lane = lax.broadcasted_iota(jnp.int32, (256, 128), 1)
    slots = jnp.tile(passage_slot.reshape(256, 16), (1, 8))
    number = lax.broadcasted_iota(jnp.int32, (256, 128), 0) // 8 + 1
    entry = jnp.where((lane < 96) & (lane // 16 == rank[:, None]), slots, 0)
    entry = jnp.where(lane == ROW_LANE + rank[:, None], number, entry)
    table = lax.dot_general(onehot_b, entry.astype(jnp.bfloat16), (((0,), (0,)), ((), ())),
                            preferred_element_type=jnp.float32).astype(jnp.bfloat16)
    table = jnp.pad(table.reshape(8, 8, 128), ((0, 0), (0, 8), (0, 0)))
    pair = jnp.concatenate([queries, pair], axis=1)
    rest = lax.ppermute(pair, "group", [(0, 3), (3, 0), (1, 2), (2, 1)])
    whole = jnp.concatenate([pair, rest], axis=1).reshape(64, 16, 128)
    whole = jnp.concatenate([whole, table], axis=0)
    whole, _ = lax.optimization_barrier((whole, home[:16]))

    up1 = shift(whole, "z", NZ, 1)
    down1 = shift(whole, "z", NZ, -1)
    up2 = shift(up1, "z", NZ, 1)
    down2 = shift(down1, "z", NZ, -1)

    distance = jnp.array([0, 1, -1, 2, -2, 3, -3, 4], jnp.int32)
    origin = jnp.mod(z - distance, NZ)
    step = jnp.array([0, 0, -1, 1, -1, 1, 2, 2], jnp.int32)
    other = jnp.array([1, 0, 0, 0, 1, 1, 0, 1], jnp.int32)
    block = jnp.mod(x + step, NX) * NC + jnp.bitwise_xor(core, other)
    ids = jnp.concatenate([origin, block, z[None]])

    early, late = (0, 1, 2, 3), (4, 5, 6, 7)
    out = score(0, early, ids, [home, own], [whole, up1, down1, up2], cost=0)
    up3 = shift(up2, "z", NZ, 1)
    down3 = shift(down2, "z", NZ, -1)
    up3, down3, after, before, out = lax.optimization_barrier((up3, down3, after, before, out))
    after_other = swap(after)
    before_other = swap(before)
    up4 = shift(up3, "z", NZ, 1)
    opposite = shift(after, "x", NX, 1)
    tokens = [whole, up1, down1, up2, down2]
    out = score(2, early, ids, [after, before, after_other, before_other], tokens[:4], out)
    up4, out = lax.optimization_barrier((up4, out))
    tokens = tokens + [up3, down3, up4]
    out = score(0, late, ids, [home, own, after, before, after_other, before_other], tokens[4:], out)
    opposite, out = lax.optimization_barrier((opposite, out))
    facing = swap(opposite)
    out = score(6, early + late, ids, [opposite], tokens, out)
    last = score(7, early + late, ids, [facing], tokens, out)
    back = lax.all_to_all(last, "z", split_axis=0, concat_axis=0, tiled=True)
    flat = back[:, :, :96].reshape(64 * RANKS, 16)
    picked = flat[targets * RANKS + rank]
    return picked.reshape(1, 32, 8, 16)


def solution(mesh):
    fine = Mesh(mesh.devices.reshape(4, NZ, NX, NC), ("group", "z", "x", "core"))
    shard = ("z", "x", "core")
    in_specs = (
        P(shard, "group", None),
        P(("group",) + shard, None, None),
        P(("group",) + shard),
        P("group", shard, None),
        P("group", shard, None, None),
    )
    out_specs = P("group", shard, None, None)
    return jax.shard_map(per_device, mesh=fine, in_specs=in_specs, out_specs=out_specs, check_vma=False)
```

```python
import functools
import jax
import jax.numpy as jnp
from jax import lax
from jax.experimental import pallas as pl
from jax.experimental.pallas import tpu as pltpu
from jax.sharding import Mesh, PartitionSpec as P

NZ, NX, NC = 8, 4, 2
RANKS = 6
NT = (((1,), (1,)), ((), ()))
ROW_LANE = 96
CHUNK = 1024


def score_kernel(first, sources, chained, *refs):
    many = len(sources)
    out, blocks, words, best, table_v, table_s, sems = refs[-7:]
    count = blocks.shape[0]
    ids = refs[0]
    inputs = refs[1:1 + count]
    tokens = refs[1 + count:1 + count + many]
    copies = [pltpu.make_async_copy(inputs[b], blocks.at[b], sems.at[b]) for b in range(count)]
    for copy in copies:
        copy.start()
    if chained:
        out[...] = refs[1 + count + many][...]
    width = 32 * many
    lane = lax.broadcasted_iota(jnp.int32, (many, 128), 1)
    origin = [ids[s] for s in sources]
    for s in range(many):
        mine = tokens[s][64 + ids[16]].astype(jnp.float32)
        table_v[s] = mine[:8].astype(jnp.int32)
    scalars = pltpu.make_async_copy(table_v, table_s, sems.at[count])
    scalars.start()
    scalars.wait()

    def work(b, block, rows, ranks):
        for i in range(ranks):
            for s in range(many):
                row = jnp.maximum(rows[i][s] - 1, 0)
                start = i * width + s * 32
                words[start:start + 16, :] = tokens[s][2 * row]
                words[start + 16:start + 32, :] = tokens[s][2 * row + 1]
        stop = ranks * width
        held = words[:stop, :]
        for c in range(0, 4096, CHUNK):
            similar = lax.dot_general(blocks[b, c:c + CHUNK, :], held, NT, preferred_element_type=jnp.float32)
            best[c // 64:(c + CHUNK) // 64, :stop] = jnp.max(similar.reshape(CHUNK // 64, 64, stop), axis=1)
        value = best[:, :stop]
        picks = (ranks * many, stop)
        ones = (lax.broadcasted_iota(jnp.int32, picks, 1) // 32
                == lax.broadcasted_iota(jnp.int32, picks, 0)).astype(jnp.bfloat16)
        total = jnp.zeros((ranks * many, 64), jnp.float32)
        for _ in range(2):
            piece = value.astype(jnp.bfloat16)
            total += lax.dot_general(ones, piece, NT, preferred_element_type=jnp.float32)
            value = value - piece.astype(jnp.float32)
        total = total * jnp.float32(1.0 / 32)
        total = jnp.concatenate([total, total], axis=1)
        index = jnp.concatenate([table_v[s, pl.ds(block, 1), :] for s in range(many)], axis=0)
        index = jnp.bitwise_and(index, 63)
        result = jnp.zeros((many, 128), jnp.float32)
        for i in range(ranks):
            found = jnp.take_along_axis(total[i * many:(i + 1) * many], index, axis=1)
            result = jnp.where(lane // 16 == i, found, result)
        for s in range(many):
            out[origin[s], pl.ds(block, 1), :] = result[s:s + 1]

    @pl.loop(0, count)
    def _(b):
        for k in range(count):
            @pl.when(b == k)
            def _():
                copies[k].wait()
        block = ids[8 + first + b]
        rows = [[table_s[s, block, ROW_LANE + i] for s in range(many)]
                for i in range(RANKS)]
        used = [functools.reduce(lambda p, q: p + q, rows[i] + rows[i + 1]) > 0 for i in range(0, RANKS, 2)]

        @pl.when(used[2])
        def _():
            work(b, block, rows, 6)

        @pl.when(jnp.logical_and(used[1], jnp.logical_not(used[2])))
        def _():
            work(b, block, rows, 4)

        @pl.when(jnp.logical_and(used[0], jnp.logical_not(used[1])))
        def _():
            work(b, block, rows, 2)


def score(first, sources, ids, passages, tokens, previous=None, cost=1):
    smem = pl.BlockSpec(memory_space=pltpu.SMEM)
    vmem = pl.BlockSpec(memory_space=pltpu.VMEM)
    held = pl.BlockSpec(memory_space=pl.ANY)
    many, count = len(sources), len(passages)
    operands = [ids, *passages, *tokens]
    specs = [smem] + [held] * count + [vmem] * many
    if previous is not None:
        operands.append(previous)
        specs.append(vmem)
    live = count * 4096 * 32 * many * RANKS
    return pl.pallas_call(
        functools.partial(score_kernel, first, sources, previous is not None),
        in_specs=specs,
        out_specs=vmem,
        out_shape=jax.ShapeDtypeStruct((8, 8, 128), jnp.float32),
        scratch_shapes=[
            pltpu.VMEM((count, 4096, 128), jnp.bfloat16),
            pltpu.VMEM((RANKS * 32 * many, 128), jnp.bfloat16),
            pltpu.VMEM((64, RANKS * 32 * many), jnp.float32),
            pltpu.VMEM((many, 8, 128), jnp.int32),
            pltpu.SMEM((many, 8, 128), jnp.int32),
            pltpu.SemaphoreType.DMA((count + 1,)),
        ],
        compiler_params=pltpu.CompilerParams(vmem_limit_bytes=16 * 2**20),
        cost_estimate=pl.CostEstimate(flops=cost * 128 * live, bytes_accessed=2**20, transcendentals=0),
    )(*operands)


def fill_kernel(lengths, passages, out):
    position = lax.broadcasted_iota(jnp.int32, (64, 128), 0)
    for j in range(64):
        value = passages[j].astype(jnp.float32)
        value = jnp.where(position < lengths[j], value, value[:1])
        out[j * 64:(j + 1) * 64, :] = value.astype(jnp.bfloat16)


def fill(lengths, passages):
    return pl.pallas_call(
        fill_kernel,
        in_specs=[pl.BlockSpec(memory_space=pltpu.SMEM), pl.BlockSpec(memory_space=pltpu.VMEM)],
        out_specs=pl.BlockSpec(memory_space=pltpu.VMEM),
        out_shape=jax.ShapeDtypeStruct((4096, 128), jnp.bfloat16),
        cost_estimate=pl.CostEstimate(flops=2**20, bytes_accessed=2**21, transcendentals=0),
    )(lengths, passages)


def shift(value, axis, size, by):
    return lax.ppermute(value, axis, [(i, (i + by) % size) for i in range(size)])


def per_device(queries, passages, lengths, target_shard, passage_slot):
    z, x, core = lax.axis_index("z"), lax.axis_index("x"), lax.axis_index("core")
    pair = lax.ppermute(queries, "group", [(0, 1), (1, 0), (2, 3), (3, 2)])
    own = fill(lengths, passages)
    swap = lambda value: lax.ppermute(value, "core", [(0, 1), (1, 0)])
    pair, own = lax.optimization_barrier((pair, own))
    home = swap(own)
    after = shift(own, "x", NX, 1)
    before = shift(own, "x", NX, -1)

    targets = target_shard.reshape(256)
    onehot = (targets[:, None] == lax.broadcasted_iota(jnp.int32, (256, 64), 1))
    triangle = (lax.broadcasted_iota(jnp.int32, (256, 256), 0)
                > lax.broadcasted_iota(jnp.int32, (256, 256), 1)).astype(jnp.bfloat16)
    onehot_b = onehot.astype(jnp.bfloat16)
    earlier = jnp.dot(triangle, onehot_b, preferred_element_type=jnp.float32)
    rank = jnp.sum(jnp.where(onehot, earlier, 0.0), axis=1).astype(jnp.int32)
    lane = lax.broadcasted_iota(jnp.int32, (256, 128), 1)
    slots = jnp.tile(passage_slot.reshape(256, 16), (1, 8))
    number = lax.broadcasted_iota(jnp.int32, (256, 128), 0) // 8 + 1
    entry = jnp.where((lane < 96) & (lane // 16 == rank[:, None]), slots, 0)
    entry = jnp.where(lane == ROW_LANE + rank[:, None], number, entry)
    table = lax.dot_general(onehot_b, entry.astype(jnp.bfloat16), (((0,), (0,)), ((), ())),
                            preferred_element_type=jnp.float32).astype(jnp.bfloat16)
    table = jnp.pad(table.reshape(8, 8, 128), ((0, 0), (0, 8), (0, 0)))
    pair = jnp.concatenate([queries, pair], axis=1)
    rest = lax.ppermute(pair, "group", [(0, 3), (3, 0), (1, 2), (2, 1)])
    whole = jnp.concatenate([pair, rest], axis=1).reshape(64, 16, 128)
    whole = jnp.concatenate([whole, table], axis=0)
    whole, _ = lax.optimization_barrier((whole, home[:16]))

    up1 = shift(whole, "z", NZ, 1)
    down1 = shift(whole, "z", NZ, -1)
    up2 = shift(up1, "z", NZ, 1)
    down2 = shift(down1, "z", NZ, -1)

    distance = jnp.array([0, 1, -1, 2, -2, 3, -3, 4], jnp.int32)
    origin = jnp.mod(z - distance, NZ)
    step = jnp.array([0, 0, -1, 1, -1, 1, 2, 2], jnp.int32)
    other = jnp.array([1, 0, 0, 0, 1, 1, 0, 1], jnp.int32)
    block = jnp.mod(x + step, NX) * NC + jnp.bitwise_xor(core, other)
    ids = jnp.concatenate([origin, block, z[None]])

    early, late = (0, 1, 2, 3), (4, 5, 6, 7)
    out = score(0, early, ids, [home, own], [whole, up1, down1, up2], cost=0)
    up3 = shift(up2, "z", NZ, 1)
    down3 = shift(down2, "z", NZ, -1)
    up3, down3, after, before, out = lax.optimization_barrier((up3, down3, after, before, out))
    after_other = swap(after)
    before_other = swap(before)
    up4 = shift(up3, "z", NZ, 1)
    opposite = shift(after, "x", NX, 1)
    tokens = [whole, up1, down1, up2, down2]
    out = score(2, early, ids, [after, before], tokens[:4], out)
    out = score(4, early, ids, [after_other, before_other], tokens[:4], out)
    up4, out = lax.optimization_barrier((up4, out))
    tokens = tokens + [up3, down3, up4]
    out = score(0, late, ids, [home, own, after, before, after_other, before_other], tokens[4:], out)
    opposite, out = lax.optimization_barrier((opposite, out))
    facing = swap(opposite)
    out = score(6, early + late, ids, [opposite], tokens, out)
    last = score(7, early + late, ids, [facing], tokens, out)
    back = lax.all_to_all(last, "z", split_axis=0, concat_axis=0, tiled=True)
    flat = back[:, :, :96].reshape(64 * RANKS, 16)
    picked = flat[targets * RANKS + rank]
    return picked.reshape(1, 32, 8, 16)


def solution(mesh):
    fine = Mesh(mesh.devices.reshape(4, NZ, NX, NC), ("group", "z", "x", "core"))
    shard = ("z", "x", "core")
    in_specs = (
        P(shard, "group", None),
        P(("group",) + shard, None, None),
        P(("group",) + shard),
        P("group", shard, None),
        P("group", shard, None, None),
    )
    out_specs = P("group", shard, None, None)
    return jax.shard_map(per_device, mesh=fine, in_specs=in_specs, out_specs=out_specs, check_vma=False)
```
